768 devices in a mesh: row: 8 (over z_lo, core), col: 12 (over z_hi, x), depth: 8 (over y).
Axes of the slice: x: 4, y: 8, z: 12 (z_hi: 3, z_lo: 4; z = z_hi * 4 + z_lo), core: 2. Of those that a mesh axis runs over, the one named last changes fastest.
Arguments:
- left_blocks: float32 [12288, 64, 64], P(('row', 'col', 'depth')), may hold values from -6 to 6
- right_blocks: float32 [12288, 64, 64], P(('row', 'col', 'depth')), may hold values from -0.125 to 0.125
- triples: int32 [3, 393216], P(None, ('row', 'col', 'depth')), may hold values from 0 to 191, as said below
Outputs:
- product_blocks: float32 [12288, 64, 64], P(('row', 'col', 'depth'))
The draws below stay inside these ranges and needn't reach their ends.
Inputs may be any that keep to these rules, and one draw needn't show every extreme that they name: With G = 4 contraction groups per panel and layer, left slot number i * G + g is the block of block row i and group g, and right slot j * G + g the block of group g and block column j. Each device keeps 128 distinct (block row, block column) pairs, and out slot o names the o-th of them. A used triple takes the left block (i, g) and the right block (g, j) of one group g and sends their product to the kept slot of (i, j); a device's used triples are distinct and come first among its 512. An unused triple is (0, 0, 128). Every device has at least 128 used triples, and some device has all 512 used.
All inputs are finite; a program needn't handle non-finite values.
Results may differ from the reference program's by a relative error of at most 0.0003.
Values sent between devices are 32-bit elements; how exact they have to be, the bound alone decides.
No kernel may reach another device: no remote copies, remote signals or barrier semaphores. Data moves between devices by JAX's collectives and lax.ppermute only.
A program may use at most 128 MiB of HBM per device.

```python
import jax
import jax.numpy as jnp
from jax import lax

BS = 64
SA = 16
PC = 128
MAXT = 512
A_BLOCKS = 12288
N_ROW = 8
N_COL = 12
N_DEPTH = 8
DEVICES = 768


def draw_triples(key, part):
    key = jax.random.fold_in(key, 7)
    groups = max(1, SA // 4)
    block_rows = N_COL * SA // groups
    block_cols = N_ROW * SA // groups
    pair_total = block_rows * block_cols
    cand_total = PC * groups
    key_pairs, key_cands, key_live = jax.random.split(key, 3)
    pair_keys = jax.random.split(key_pairs, DEVICES)
    cand_keys = jax.random.split(key_cands, DEVICES)
    pairs = jax.vmap(lambda one: jax.random.permutation(one, pair_total))(pair_keys)
    pairs = (pairs - pairs[:, :1] + pair_total - 1) % pair_total
    pairs = pairs[:, :PC]
    cands = jax.vmap(lambda one: jax.random.permutation(one, cand_total))(cand_keys)
    cands = (cands - cands[:, :1] + groups - 1) % cand_total
    cands = cands[:, :MAXT]
    out_slot = cands // groups
    group_at = cands % groups
    chosen = jnp.take_along_axis(pairs, out_slot, axis=1)
    row_at = chosen // block_cols
    col_at = chosen % block_cols
    left_slot = row_at * groups + group_at
    right_slot = col_at * groups + group_at
    live_count = jax.random.randint(key_live, (DEVICES,), MAXT // 4, MAXT + 1)
    live_count = live_count.at[0].set(MAXT)
    live_count = live_count.at[DEVICES - 1].set(MAXT // 4)
    position = jnp.arange(MAXT)
    keep = position[None, :] < live_count[:, None]
    left_slot = jnp.where(keep, left_slot, 0)
    right_slot = jnp.where(keep, right_slot, 0)
    out_slot = jnp.where(keep, out_slot, PC)
    stacked = jnp.stack([left_slot.reshape(-1), right_slot.reshape(-1), out_slot.reshape(-1)])
    return stacked.astype(jnp.int32)


def block_scale(key, dims, shards, smallest, top_value):
    def one(dim, shards_of):
        steps = jax.random.uniform(jax.random.fold_in(jax.random.fold_in(key, 6), dim), (shards_of,), jnp.float32, smallest / len(shards), top_value / len(shards))
        return jnp.repeat(jnp.exp(steps), dims[dim] // shards_of).reshape((-1,) + (1,) * (len(dims) - dim - 1))

    factor_of = one(*shards[0])
    for cut in shards[1:]:
        factor_of = factor_of * one(*cut)
    return factor_of


def noise(own_key, shape, deviation, most, cuts=(), kind=jnp.bfloat16):
    entries = deviation * jax.random.normal(own_key, shape, jnp.float32)
    if cuts:
        entries = entries * block_scale(own_key, shape, cuts, -0.22, 0.18)
    return jnp.clip(entries, -most, most).astype(kind)


def setup_inputs(seed: int = 0) -> dict:
    key_list = jax.random.split(jax.random.key(seed), 4)
    return {
        "left_blocks": noise(key_list[0], (A_BLOCKS, BS, BS), 1.0, 6.0, ((0, 768),), jnp.float32),
        "right_blocks": noise(key_list[1], (A_BLOCKS, BS, BS), (BS * MAXT * N_DEPTH // PC) ** -0.5, 0.125, ((0, 768),), jnp.float32),
        "triples": draw_triples(jax.random.fold_in(key_list[3], 71), 0),
    }


def reference(left_blocks, right_blocks, triples):
    left_all = left_blocks.reshape(N_ROW, N_COL, N_DEPTH, SA, BS, BS)
    right_all = right_blocks.reshape(N_ROW, N_COL, N_DEPTH, SA, BS, BS)
    slot_all = triples.reshape(3, N_ROW, N_COL, N_DEPTH, MAXT)

    def one_panel(flat):
        row_at = flat // N_COL
        col_at = flat % N_COL

        def layer(total, depth_at):
            left_panel = left_all[row_at, :, depth_at].reshape(N_COL * SA, BS, BS)
            right_panel = right_all[:, col_at, depth_at].reshape(N_ROW * SA, BS, BS)
            picks = slot_all[:, row_at, col_at, depth_at]
            products = jnp.einsum("tij,tjk->tik", left_panel[picks[0]], right_panel[picks[1]], precision=lax.Precision.HIGHEST, preferred_element_type=jnp.float32)
            return total.at[picks[2]].add(products), None

        start_total = jnp.zeros((PC + 1, BS, BS), jnp.float32)
        total, unused = lax.scan(layer, start_total, jnp.arange(N_DEPTH, dtype=jnp.int32))
        return total[:PC]

    panels = lax.map(one_panel, jnp.arange(N_ROW * N_COL, dtype=jnp.int32))
    return panels.reshape(N_ROW * N_COL * PC, BS, BS)
```

```python
import jax
import jax.numpy as jnp
from jax import lax
from jax.experimental import pallas as pl
from jax.experimental.pallas import tpu as pltpu
from jax.sharding import PartitionSpec as P

BS = 64
GROUPS = 4
SLOTS = 512
PC = 128
LAYERS = 8
SHARE = PC // LAYERS
VM = pl.BlockSpec(memory_space=pltpu.VMEM)
SM = pl.BlockSpec(memory_space=pltpu.SMEM)
F32 = jnp.float32
BF16 = jnp.bfloat16


def params():
    return pltpu.CompilerParams(vmem_limit_bytes=32 * 2**20)


def cost(flops, nbytes):
    return pl.CostEstimate(flops=flops, bytes_accessed=nbytes, transcendentals=0)


def pack_kernel(l_ref, r_ref, lp_ref, rp_ref):
    for i in range(4):
        for h in range(2):
            lp_ref[i * 64 : (i + 1) * 64, h * 128 : (h + 1) * 128] = jnp.concatenate(
                [l_ref[4 * i + 2 * h], l_ref[4 * i + 2 * h + 1]], axis=1
            )
    for g in range(GROUPS):
        for h in range(2):
            rp_ref[g * 64 : (g + 1) * 64, h * 128 : (h + 1) * 128] = jnp.concatenate(
                [r_ref[8 * h + g], r_ref[8 * h + 4 + g]], axis=1
            )


def pack(l, r):
    o = jax.ShapeDtypeStruct((256, 256), F32)
    return pl.pallas_call(
        pack_kernel, out_shape=(o, o), in_specs=[VM, VM], out_specs=(VM, VM), compiler_params=params(), cost_estimate=cost(0, 2**21)
    )(l, r)


def table_kernel(t_ref, o_ref):
    def clear(k, c):
        o_ref[k] = 0
        return c

    lax.fori_loop(0, 136, clear, 0, unroll=8)

    def put(t, c):
        a = t_ref[0, t]
        b = t_ref[1, t]
        k = t_ref[2, t]
        o_ref[k] = o_ref[k] | (a >> 2) | ((b >> 2) << 8) | (1 << (16 + (a & 3)))
        return c

    lax.fori_loop(0, SLOTS, put, 0, unroll=8)


def table(t):
    return pl.pallas_call(
        table_kernel,
        out_shape=jax.ShapeDtypeStruct((136,), jnp.int32),
        in_specs=[SM],
        out_specs=SM, compiler_params=params(),
        cost_estimate=cost(0, 2**23),
    )(t)


def prep_left(x, ls, at):
    for i in range(4):
        v = x[i * 64 : (i + 1) * 64, :]
        hi = v.astype(BF16)
        ls[at * 4 + i, 0:64, :] = hi
        ls[at * 4 + i, 64:128, :] = (v - hi.astype(F32)).astype(BF16)


def prep_right(x, rs, at):
    lane = lax.broadcasted_iota(jnp.int32, (64, 128), 1)
    for h in range(2):
        for g in range(GROUPS):
            v = x[g * 64 : (g + 1) * 64, h * 128 : (h + 1) * 128]
            hi = v.astype(BF16).astype(F32)
            lo = pltpu.roll(v - hi, 64, 1)
            rs[at * 4 + 2 * h, g * 64 : (g + 1) * 64, :] = jnp.where(lane < 64, hi, lo).astype(BF16)
            rs[at * 4 + 2 * h + 1, g * 64 : (g + 1) * 64, :] = jnp.where(lane < 64, lo, hi).astype(BF16)


def one_slot(word, ls, rs):
    i = word & 255
    j = (word >> 8) & 255
    g = lax.broadcasted_iota(jnp.int32, (1, 256), 1) // 64
    used = (((word >> 16) >> g) & 1).astype(F32).astype(BF16)
    p = jnp.dot(ls[i] * used, rs[j], preferred_element_type=F32)
    return p[:64] + p[64:]


def two_slots(k, tab, ls, rs):
    xa = one_slot(tab[k], ls, rs)
    xb = one_slot(tab[k + 1], ls, rs)
    lane = lax.broadcasted_iota(jnp.int32, (64, 128), 1)
    u = jnp.where(lane < 64, xa, xb)
    v = jnp.where(lane < 64, xb, xa)
    return u + pltpu.roll(v, 64, 1)


def share_into(tab, first, o_ref, at, count, ls, rs):
    def step(p, c):
        for q in range(4):
            n = p * 4 + q
            o_ref[pl.ds(at + n * 64, 64), :] = two_slots(first + 2 * n, tab, ls, rs)
        return c

    lax.fori_loop(0, count // 4, step, 0)


def first_kernel(where, tab, l0, lz1, lz2, la0, lb0, lc0, la, lb, lc, r4, s4, p3, m3, f0, f1, ls, rs):
    me, col, row = where[0], where[1], where[2]
    z, x = col >> 2, col & 3

    def at(dz, dx):
        return lax.rem(z + 3 - dz, 3) * 4 + ((x + 4 - dx) & 3)

    prep_left(l0, ls, at(0, 0))
    prep_left(lz1, ls, at(1, 0))
    prep_left(lz2, ls, at(2, 0))
    prep_left(la0, ls, at(0, 1))
    prep_left(lb0, ls, at(0, 3))
    prep_left(lc0, ls, at(0, 2))
    for h in range(2):
        prep_left(la.at[pl.ds(h * 256, 256)], ls, at(1 + h, 1))
        prep_left(lb.at[pl.ds(h * 256, 256)], ls, at(1 + h, 3))
        prep_left(lc.at[pl.ds(h * 256, 256)], ls, at(1 + h, 2))
    zl, core = row >> 1, row & 1
    for k in range(4):
        prep_right(r4.at[pl.ds(k * 256, 256)], rs, ((zl + 4 - k) & 3) * 2 + core)
        prep_right(s4.at[pl.ds(k * 256, 256)], rs, ((zl + 4 - k) & 3) * 2 + 1 - core)

    def share(k):
        return ((me + 8 + k) & 7) * SHARE

    share_into(tab, share(3), p3, 0, 8, ls, rs)
    share_into(tab, share(1), p3, 512, 8, ls, rs)
    share_into(tab, share(-3), m3, 0, 8, ls, rs)
    share_into(tab, share(-1), m3, 512, 8, ls, rs)
    share_into(tab, share(4), f0, 0, 4, ls, rs)
    share_into(tab, share(4) + 8, f1, 0, 4, ls, rs)


def first(where, tab, parts):
    two = jax.ShapeDtypeStruct((1024, 128), F32)
    half = jax.ShapeDtypeStruct((256, 128), F32)
    return pl.pallas_call(
        first_kernel,
        out_shape=(
            two,
            two,
            half,
            half,
            jax.ShapeDtypeStruct((48, 128, 256), BF16),
            jax.ShapeDtypeStruct((32, 256, 128), BF16),
        ),
        in_specs=[SM, SM] + [VM] * len(parts),
        out_specs=(VM,) * 6,
        compiler_params=params(),
        cost_estimate=cost(2**30, 2**24),
    )(where, tab, *parts)


def second_kernel(where, tab, ls, rs, up, dn, own):
    me = where[0]

    def share(k):
        return ((me + 8 + k) & 7) * SHARE

    share_into(tab, share(2), up, 0, 8, ls, rs)
    share_into(tab, share(-2), dn, 0, 8, ls, rs)
    share_into(tab, share(0), own, 0, 8, ls, rs)


def second(where, tab, ls, rs):
    o = jax.ShapeDtypeStruct((512, 128), F32)
    return pl.pallas_call(
        second_kernel,
        out_shape=(o, o, o),
        in_specs=[SM, SM, VM, VM],
        out_specs=(VM, VM, VM),
        compiler_params=params(),
        cost_estimate=cost(2**29, 2**23),
    )(where, tab, ls, rs)


def middle_kernel(up, dn, q1, q2, q3, q4, u, d):
    u[0:256, :] = up[0:256, :] + q1[0:256, :] + q3[...]
    u[256:512, :] = up[256:512, :] + q1[256:512, :]
    d[0:256, :] = dn[0:256, :] + q2[0:256, :]
    d[256:512, :] = dn[256:512, :] + q2[256:512, :] + q4[...]


def middle(*a):
    o = jax.ShapeDtypeStruct((512, 128), F32)
    return pl.pallas_call(
        middle_kernel, out_shape=(o, o), in_specs=[VM] * 6, compiler_params=params(), out_specs=(VM, VM), cost_estimate=cost(0, 2**21)
    )(*a)


def last_kernel(own, q1, q2, u, d, o_ref):
    for p in range(8):
        s = slice(p * 64, (p + 1) * 64)
        t = slice(512 + p * 64, 512 + (p + 1) * 64)
        v = own[s, :] + q1[t, :] + q2[t, :] + u[s, :] + d[s, :]
        o_ref[2 * p] = v[:, 0:64]
        o_ref[2 * p + 1] = v[:, 64:128]


def last(*a):
    return pl.pallas_call(
        last_kernel,
        out_shape=jax.ShapeDtypeStruct((SHARE, BS, BS), F32),
        in_specs=[VM] * 5, compiler_params=params(),
        out_specs=VM,
        cost_estimate=cost(0, 2**21),
    )(*a)


def along_col(x, dz, dx):
    return lax.ppermute(
        x, "col", [(z * 4 + c, (z + dz) % 3 * 4 + (c + dx) % 4) for z in range(3) for c in range(4)]
    )


def along_row(x, dz, dc):
    return lax.ppermute(
        x, "row", [(z * 2 + c, (z + dz) % 4 * 2 + (c + dc) % 2) for z in range(4) for c in range(2)]
    )


def along_depth(x, k):
    return lax.ppermute(x, "depth", [(i, (i + k) % LAYERS) for i in range(LAYERS)])


def pass_on(a, b):
    h = a.shape[0] // 2
    return jnp.concatenate([along_col(a[:h], 0, 1), along_col(b[h:], 0, -1)])


def per_device(left_blocks, right_blocks, triples):
    me = lax.axis_index("depth")
    where = jnp.stack([me, lax.axis_index("col"), lax.axis_index("row")]).astype(jnp.int32)
    l, r = pack(left_blocks, right_blocks)
    tab = table(triples)
    lz1, lz2 = along_col(l, 1, 0), along_col(l, 2, 0)
    la0, lb0 = along_col(l, 0, 1), along_col(l, 0, -1)
    lc0 = pass_on(la0, lb0)
    lz1, lz2, r = lax.optimization_barrier((lz1, lz2, r))
    l2 = jnp.concatenate([lz1, lz2])
    la, lb = along_col(l2, 0, 1), along_col(l2, 0, -1)
    r4 = jnp.concatenate([r] + [along_row(r, k, 0) for k in (1, 2, 3)])
    la, lb = lax.optimization_barrier((la, lb))
    h = 128
    up_half = along_col(jnp.concatenate([la[:h], la[256 : 256 + h]]), 0, 1)
    dn_half = along_col(jnp.concatenate([lb[h:256], lb[256 + h :]]), 0, -1)
    lc = jnp.concatenate([up_half[:h], dn_half[:h], up_half[h:], dn_half[h:]])
    s4 = along_row(r4, 0, 1)
    p3, m3, f0, f1, ls, rs = first(where, tab, (l, lz1, lz2, la0, lb0, lc0, la, lb, lc, r4, s4))
    q1, q2 = along_depth(p3, 1), along_depth(m3, -1)
    q3, q4 = along_depth(f0, 2), along_depth(f1, -2)
    up, dn, own = second(where, tab, ls, rs)
    u, d = middle(up, dn, q1, q2, q3, q4)
    u, d = along_depth(u, 2), along_depth(d, -2)
    return last(own, q1, q2, u, d)


def solution(mesh):
    placed = (
        P(("row", "col", "depth"), None, None),
        P(("row", "col", "depth"), None, None),
        P(None, ("row", "col", "depth")),
    )
    return jax.shard_map(
        per_device,
        mesh=mesh,
        in_specs=placed,
        out_specs=P(("row", "col", "depth"), None, None),
        check_vma=False,
    )
```

```python
import jax
import jax.numpy as jnp
from jax import lax
from jax.experimental import pallas as pl
from jax.experimental.pallas import tpu as pltpu
from jax.sharding import PartitionSpec as P

BS = 64
GROUPS = 4
SLOTS = 512
PC = 128
LAYERS = 8
SHARE = PC // LAYERS
VM = pl.BlockSpec(memory_space=pltpu.VMEM)
SM = pl.BlockSpec(memory_space=pltpu.SMEM)
F32 = jnp.float32
BF16 = jnp.bfloat16


def params():
    return pltpu.CompilerParams(vmem_limit_bytes=16 * 2**20)


def cost(flops, nbytes):
    return pl.CostEstimate(flops=flops, bytes_accessed=nbytes, transcendentals=0)


def pack_left_kernel(l_ref, three_ref, one_ref):
    for i in range(4):
        for h in range(2):
            v = jnp.concatenate([l_ref[4 * i + 2 * h], l_ref[4 * i + 2 * h + 1]], axis=1)
            at = (slice(i * 64, (i + 1) * 64), slice(h * 128, (h + 1) * 128))
            for c in range(3):
                three_ref[(c,) + at] = v
            one_ref[at] = v


def pack_left(l):
    return pl.pallas_call(
        pack_left_kernel,
        out_shape=(jax.ShapeDtypeStruct((3, 256, 256), F32), jax.ShapeDtypeStruct((256, 256), F32)),
        in_specs=[VM],
        out_specs=(VM, VM),
        compiler_params=params(),
        cost_estimate=cost(0, 2**21),
    )(l)


def pack_right_kernel(r_ref, o_ref):
    for g in range(GROUPS):
        for h in range(2):
            o_ref[g * 64 : (g + 1) * 64, h * 128 : (h + 1) * 128] = jnp.concatenate(
                [r_ref[8 * h + g], r_ref[8 * h + 4 + g]], axis=1
            )


def pack_right(r):
    return pl.pallas_call(
        pack_right_kernel,
        out_shape=jax.ShapeDtypeStruct((256, 256), F32),
        in_specs=[VM],
        out_specs=VM,
        compiler_params=params(),
        cost_estimate=cost(0, 2**21),
    )(r)


def table_kernel(t_ref, o_ref):
    def clear(k, c):
        o_ref[k] = 0
        return c

    lax.fori_loop(0, 136, clear, 0, unroll=8)

    def put(t, c):
        a = t_ref[0, t]
        b = t_ref[1, t]
        k = t_ref[2, t]
        o_ref[k] = o_ref[k] | (a >> 2) | ((b >> 2) << 8) | (1 << (16 + (a & 3)))
        return c

    lax.fori_loop(0, SLOTS, put, 0, unroll=8)


def table(t):
    return pl.pallas_call(
        table_kernel,
        out_shape=jax.ShapeDtypeStruct((136,), jnp.int32),
        in_specs=[SM],
        out_specs=SM, compiler_params=params(),
        cost_estimate=cost(0, 2**23),
    )(t)


def prep_left(x, ls, at):
    for i in range(4):
        v = x[i * 64 : (i + 1) * 64, :]
        hi = v.astype(BF16)
        ls[at * 4 + i, 0:64, :] = hi
        ls[at * 4 + i, 64:128, :] = (v - hi.astype(F32)).astype(BF16)


def prep_right(x, rs, at):
    lane = lax.broadcasted_iota(jnp.int32, (64, 128), 1)
    for h in range(2):
        for g in range(GROUPS):
            v = x[g * 64 : (g + 1) * 64, h * 128 : (h + 1) * 128]
            hi = v.astype(BF16).astype(F32)
            lo = pltpu.roll(v - hi, 64, 1)
            rs[at * 4 + 2 * h, g * 64 : (g + 1) * 64, :] = jnp.where(lane < 64, hi, lo).astype(BF16)
            rs[at * 4 + 2 * h + 1, g * 64 : (g + 1) * 64, :] = jnp.where(lane < 64, lo, hi).astype(BF16)


def one_slot(word, ls, rs):
    i = word & 255
    j = (word >> 8) & 255
    g = lax.broadcasted_iota(jnp.int32, (1, 256), 1) // 64
    used = (((word >> 16) >> g) & 1).astype(F32).astype(BF16)
    p = jnp.dot(ls[i] * used, rs[j], preferred_element_type=F32)
    return p[:64] + p[64:]


def two_slots(k, tab, ls, rs):
    xa = one_slot(tab[k], ls, rs)
    xb = one_slot(tab[k + 1], ls, rs)
    lane = lax.broadcasted_iota(jnp.int32, (64, 128), 1)
    u = jnp.where(lane < 64, xa, xb)
    v = jnp.where(lane < 64, xb, xa)
    return u + pltpu.roll(v, 64, 1)


def share_into(tab, first, o_ref, at, count, ls, rs):
    def step(p, c):
        for q in range(4):
            n = p * 4 + q
            o_ref[pl.ds(at + n * 64, 64), :] = two_slots(first + 2 * n, tab, ls, rs)
        return c

    lax.fori_loop(0, count // 4, step, 0)


LEFT = jax.ShapeDtypeStruct((48, 128, 256), BF16)
RIGHT = jax.ShapeDtypeStruct((32, 256, 128), BF16)


def split_own_kernel(where, l0, la, lb, lc, ls):
    z, x = where[1] >> 2, where[1] & 3
    for k, ref in enumerate((l0, la, lb, lc)):
        prep_left(ref, ls, z * 4 + ((x + 4 - k) & 3))


def split_own(where, *parts):
    return pl.pallas_call(
        split_own_kernel,
        out_shape=LEFT,
        in_specs=[SM] + [VM] * 4,
        out_specs=VM,
        compiler_params=params(),
        cost_estimate=cost(0, 2**22),
    )(where, *parts)


def spread_kernel(where, zs, o_ref):
    z = where[1] >> 2
    for h in range(2):
        at = lax.rem(z + 1 + h, 3)
        for q in range(4):
            v = zs[at, q * 64 : (q + 1) * 64, :]
            for c in range(4):
                o_ref[c, h * 256 + q * 64 : h * 256 + (q + 1) * 64, :] = v


def spread(where, zs):
    return pl.pallas_call(
        spread_kernel,
        out_shape=jax.ShapeDtypeStruct((4, 512, 256), F32),
        in_specs=[SM, VM],
        out_specs=VM,
        compiler_params=params(),
        cost_estimate=cost(0, 2**21),
    )(where, zs)


def split_others_kernel(where, ls_in, xs, ls):
    z = where[1] >> 2
    for c in range(4):
        for h in range(2):
            prep_left(xs.at[c, pl.ds(h * 256, 256)], ls, lax.rem(z + 1 + h, 3) * 4 + c)


def split_others(where, ls, xs):
    return pl.pallas_call(
        split_others_kernel,
        out_shape=LEFT,
        in_specs=[SM, VM, VM],
        out_specs=VM,
        input_output_aliases={1: 0},
        compiler_params=params(),
        cost_estimate=cost(0, 2**22),
    )(where, ls, xs)


def first_right_kernel(where, *refs):
    r4, rs = refs[:4], refs[4]
    core = where[2] & 1
    for k in range(4):
        prep_right(r4[k], rs, (((where[2] >> 1) + 4 - k) & 3) * 2 + core)


def first_right(where, r4):
    return pl.pallas_call(
        first_right_kernel,
        out_shape=RIGHT,
        in_specs=[SM] + [VM] * 4,
        out_specs=VM,
        compiler_params=params(),
        cost_estimate=cost(0, 2**22),
    )(where, *r4)


def share_of(where, k):
    return ((where[0] + 8 + k) & 7) * SHARE


def last_right_kernel(where, rs_in, s4, rs):
    core = where[2] & 1
    for k in range(4):
        prep_right(s4.at[k], rs, (((where[2] >> 1) + 4 - k) & 3) * 2 + 1 - core)


def last_right(where, rs, s4):
    return pl.pallas_call(
        last_right_kernel,
        out_shape=RIGHT,
        in_specs=[SM, VM, VM],
        out_specs=VM,
        input_output_aliases={1: 0},
        compiler_params=params(),
        cost_estimate=cost(0, 2**22),
    )(where, rs, s4)


def shares(where, tab, ls, rs, offsets, after):
    def kernel(where, tab, ls, rs, after_ref, o_ref):
        for n, k in enumerate(offsets):
            share_into(tab, share_of(where, k), o_ref, n * 512, 8, ls, rs)

    return pl.pallas_call(
        kernel,
        out_shape=jax.ShapeDtypeStruct((512 * len(offsets), 128), F32),
        in_specs=[SM, SM, VM, VM, pl.BlockSpec(memory_space=pl.ANY)],
        out_specs=VM,
        compiler_params=params(),
        cost_estimate=cost(2**27 * len(offsets), 2**20 * len(offsets)),
    )(where, tab, ls, rs, after)


def far_kernel(where, tab, ls, rs, after_ref, f0, f1):
    share_into(tab, share_of(where, 4), f0, 0, 4, ls, rs)
    share_into(tab, share_of(where, 4) + 8, f1, 0, 4, ls, rs)


def far(where, tab, ls, rs, after):
    half = jax.ShapeDtypeStruct((256, 128), F32)
    return pl.pallas_call(
        far_kernel,
        out_shape=(half, half),
        in_specs=[SM, SM, VM, VM, pl.BlockSpec(memory_space=pl.ANY)],
        out_specs=(VM, VM),
        compiler_params=params(),
        cost_estimate=cost(2**27, 2**20),
    )(where, tab, ls, rs, after)


def up_kernel(near, q, half, o_ref):
    o_ref[0:256, :] = near[0:256, :] + q[0:256, :] + half[...]
    o_ref[256:512, :] = near[256:512, :] + q[256:512, :]


def down_kernel(near, q, half, after_ref, o_ref):
    o_ref[0:256, :] = near[512:768, :] + q[0:256, :]
    o_ref[256:512, :] = near[768:1024, :] + q[256:512, :] + half[...]


def merge(kernel, near, q, half, *after, weight):
    return pl.pallas_call(
        kernel,
        out_shape=jax.ShapeDtypeStruct((512, 128), F32),
        in_specs=[VM] * 3 + [pl.BlockSpec(memory_space=pl.ANY)] * len(after),
        out_specs=VM,
        compiler_params=params(),
        cost_estimate=cost(0, weight),
    )(near, q, half, *after)


def sum_kernel(near, q1, q2, u, o_ref):
    o_ref[...] = near[1024:1536, :] + q1[512:1024, :] + q2[512:1024, :] + u[...]


def partial_sum(*a):
    return pl.pallas_call(
        sum_kernel,
        out_shape=jax.ShapeDtypeStruct((512, 128), F32),
        in_specs=[VM] * 4,
        out_specs=VM,
        compiler_params=params(),
        cost_estimate=cost(0, 2**21),
    )(*a)


def last_kernel(part, d, o_ref):
    for p in range(8):
        s = slice(p * 64, (p + 1) * 64)
        v = part[s, :] + d[s, :]
        o_ref[2 * p] = v[:, 0:64]
        o_ref[2 * p + 1] = v[:, 64:128]


def last(part, d):
    return pl.pallas_call(
        last_kernel,
        out_shape=jax.ShapeDtypeStruct((SHARE, BS, BS), F32),
        in_specs=[VM] * 2,
        out_specs=VM,
        compiler_params=params(),
        cost_estimate=cost(0, 2**21),
    )(part, d)


def to_group(x, axis, groups):
    return lax.all_to_all(x, axis, 0, 0, axis_index_groups=groups)


Z_GROUPS = [[z * 4 + c for z in range(3)] for c in range(4)]
X_GROUPS = [[z * 4 + c for c in range(4)] for z in range(3)]


def along_x(x, k):
    return lax.ppermute(x, "col", [(z * 4 + c, z * 4 + (c + k) % 4) for z in range(3) for c in range(4)])


def along_z(x, k):
    return lax.ppermute(x, "row", [(z * 2 + c, (z + k) % 4 * 2 + c) for z in range(4) for c in range(2)])


def along_depth(x, k):
    return lax.ppermute(x, "depth", [(i, (i + k) % LAYERS) for i in range(LAYERS)])


def per_device(left_blocks, right_blocks, triples):
    me, col, row = lax.axis_index("depth"), lax.axis_index("col"), lax.axis_index("row")
    where = jnp.stack([me, col, row]).astype(jnp.int32)
    l3, l = pack_left(left_blocks)
    zs = to_group(l3, "col", Z_GROUPS)
    r = pack_right(right_blocks)
    tab = table(triples)
    own_x = [along_x(l, k) for k in (1, 2, 3)]
    ls = split_own(where, l, *own_x)
    zs, ls, tab, r, where = lax.optimization_barrier((zs, ls, tab, r, where))
    xs = to_group(spread(where, zs), "col", X_GROUPS)
    rk = [r] + [along_z(r, k) for k in (1, 2, 3)]
    ls = split_others(where, ls, xs)
    rk, ls = lax.optimization_barrier((rk, ls))
    s4 = lax.ppermute(jnp.stack(rk), "row", [(i, i ^ 1) for i in range(8)])
    rs = last_right(where, first_right(where, rk), s4)
    p3 = shares(where, tab, ls, rs, (3, 1), where)
    m3 = shares(where, tab, ls, rs, (-3, -1), p3)
    f0, f1 = far(where, tab, ls, rs, m3)
    q1, q2 = along_depth(p3, 1), along_depth(m3, -1)
    q3, q4 = along_depth(f0, 2), along_depth(f1, -2)
    near = shares(where, tab, ls, rs, (2, -2, 0), f0)
    u = merge(up_kernel, near, q1, q3, weight=2**22)
    d = merge(down_kernel, near, q2, q4, u, weight=2**20)
    u, d = along_depth(u, 2), along_depth(d, -2)
    return last(partial_sum(near, q1, q2, u), d)


def solution(mesh):
    placed = (
        P(("row", "col", "depth"), None, None),
        P(("row", "col", "depth"), None, None),
        P(None, ("row", "col", "depth")),
    )
    return jax.shard_map(
        per_device,
        mesh=mesh,
        in_specs=placed,
        out_specs=P(("row", "col", "depth"), None, None),
        check_vma=False,
    )
```

```python
import jax
import jax.numpy as jnp
from jax import lax
from jax.experimental import pallas as pl
from jax.experimental.pallas import tpu as pltpu
from jax.sharding import PartitionSpec as P

BS = 64
GROUPS = 4
SLOTS = 512
PC = 128
LAYERS = 8
SHARE = PC // LAYERS
VM = pl.BlockSpec(memory_space=pltpu.VMEM)
SM = pl.BlockSpec(memory_space=pltpu.SMEM)
F32 = jnp.float32
BF16 = jnp.bfloat16


def params():
    return pltpu.CompilerParams(vmem_limit_bytes=16 * 2**20)


def cost(flops, nbytes):
    return pl.CostEstimate(flops=flops, bytes_accessed=nbytes, transcendentals=0)


def pack_left_kernel(l_ref, three_ref, one_ref):
    for i in range(4):
        for h in range(2):
            v = jnp.concatenate([l_ref[4 * i + 2 * h], l_ref[4 * i + 2 * h + 1]], axis=1)
            at = (slice(i * 64, (i + 1) * 64), slice(h * 128, (h + 1) * 128))
            for c in range(3):
                three_ref[(c,) + at] = v
            one_ref[at] = v


def pack_left(l):
    return pl.pallas_call(
        pack_left_kernel,
        out_shape=(jax.ShapeDtypeStruct((3, 256, 256), F32), jax.ShapeDtypeStruct((256, 256), F32)),
        in_specs=[VM],
        out_specs=(VM, VM),
        compiler_params=params(),
        cost_estimate=cost(0, 2**21),
    )(l)


def pack_right_kernel(r_ref, o_ref):
    for g in range(GROUPS):
        for h in range(2):
            o_ref[g * 64 : (g + 1) * 64, h * 128 : (h + 1) * 128] = jnp.concatenate(
                [r_ref[8 * h + g], r_ref[8 * h + 4 + g]], axis=1
            )


def pack_right(r):
    return pl.pallas_call(
        pack_right_kernel,
        out_shape=jax.ShapeDtypeStruct((256, 256), F32),
        in_specs=[VM],
        out_specs=VM,
        compiler_params=params(),
        cost_estimate=cost(0, 2**21),
    )(r)


def table_kernel(t_ref, o_ref):
    def clear(k, c):
        o_ref[k] = 0
        return c

    lax.fori_loop(0, 136, clear, 0, unroll=8)

    def put(t, c):
        a = t_ref[0, t]
        b = t_ref[1, t]
        k = t_ref[2, t]
        o_ref[k] = o_ref[k] | (a >> 2) | ((b >> 2) << 8) | (1 << (16 + (a & 3)))
        return c

    lax.fori_loop(0, SLOTS, put, 0, unroll=8)


def table(t):
    return pl.pallas_call(
        table_kernel,
        out_shape=jax.ShapeDtypeStruct((136,), jnp.int32),
        in_specs=[SM],
        out_specs=SM, compiler_params=params(),
        cost_estimate=cost(0, 2**23),
    )(t)


def prep_left(x, ls, at):
    for i in range(4):
        v = x[i * 64 : (i + 1) * 64, :]
        hi = v.astype(BF16)
        ls[at * 4 + i, 0:64, :] = hi
        ls[at * 4 + i, 64:128, :] = (v - hi.astype(F32)).astype(BF16)


def prep_right(x, rs, at):
    lane = lax.broadcasted_iota(jnp.int32, (64, 128), 1)
    for h in range(2):
        for g in range(GROUPS):
            v = x[g * 64 : (g + 1) * 64, h * 128 : (h + 1) * 128]
            hi = v.astype(BF16).astype(F32)
            lo = pltpu.roll(v - hi, 64, 1)
            rs[at * 4 + 2 * h, g * 64 : (g + 1) * 64, :] = jnp.where(lane < 64, hi, lo).astype(BF16)
            rs[at * 4 + 2 * h + 1, g * 64 : (g + 1) * 64, :] = jnp.where(lane < 64, lo, hi).astype(BF16)


def one_slot(word, ls, rs):
    i = word & 255
    j = (word >> 8) & 255
    g = lax.broadcasted_iota(jnp.int32, (1, 256), 1) // 64
    used = (((word >> 16) >> g) & 1).astype(F32).astype(BF16)
    p = jnp.dot(ls[i] * used, rs[j], preferred_element_type=F32)
    return p[:64] + p[64:]


def two_slots(k, tab, ls, rs):
    xa = one_slot(tab[k], ls, rs)
    xb = one_slot(tab[k + 1], ls, rs)
    lane = lax.broadcasted_iota(jnp.int32, (64, 128), 1)
    u = jnp.where(lane < 64, xa, xb)
    v = jnp.where(lane < 64, xb, xa)
    return u + pltpu.roll(v, 64, 1)


def share_into(tab, first, o_ref, at, count, ls, rs):
    for n in range(count):
        o_ref[at + n * 64 : at + (n + 1) * 64, :] = two_slots(first + 2 * n, tab, ls, rs)


LEFT = jax.ShapeDtypeStruct((48, 128, 256), BF16)
RIGHT = jax.ShapeDtypeStruct((32, 256, 128), BF16)


def split_one(where, k, part, *so_far):
    def kernel(where, part, *rest):
        z, x = where[1] >> 2, where[1] & 3
        prep_left(part, rest[-1], z * 4 + ((x + 4 - k) & 3))

    return pl.pallas_call(
        kernel,
        out_shape=LEFT,
        in_specs=[SM] + [VM] * (1 + len(so_far)),
        out_specs=VM,
        input_output_aliases={2: 0} if so_far else {},
        compiler_params=params(),
        cost_estimate=cost(0, 2**20),
    )(where, part, *so_far)


def spread_kernel(where, zs, o_ref):
    z = where[1] >> 2
    for h in range(2):
        at = lax.rem(z + 1 + h, 3)
        for q in range(4):
            v = zs[at, q * 64 : (q + 1) * 64, :]
            for c in range(4):
                o_ref[c, h * 256 + q * 64 : h * 256 + (q + 1) * 64, :] = v


def spread(where, zs):
    return pl.pallas_call(
        spread_kernel,
        out_shape=jax.ShapeDtypeStruct((4, 512, 256), F32),
        in_specs=[SM, VM],
        out_specs=VM,
        compiler_params=params(),
        cost_estimate=cost(0, 2**21),
    )(where, zs)


def split_others_kernel(where, ls_in, xs, ls):
    z = where[1] >> 2
    for c in range(4):
        for h in range(2):
            prep_left(xs.at[c, pl.ds(h * 256, 256)], ls, lax.rem(z + 1 + h, 3) * 4 + c)


def split_others(where, ls, xs):
    return pl.pallas_call(
        split_others_kernel,
        out_shape=LEFT,
        in_specs=[SM, VM, VM],
        out_specs=VM,
        input_output_aliases={1: 0},
        compiler_params=params(),
        cost_estimate=cost(0, 2**22),
    )(where, ls, xs)


def first_right_kernel(where, r, sibling, r1, r2, r3, rs):
    z, core = where[2] >> 1, where[2] & 1
    prep_right(sibling, rs, z * 2 + 1 - core)
    for k, ref in enumerate((r, r1, r2, r3)):
        prep_right(ref, rs, ((z + 4 - k) & 3) * 2 + core)


def first_right(where, *parts):
    return pl.pallas_call(
        first_right_kernel,
        out_shape=RIGHT,
        in_specs=[SM] + [VM] * 5,
        out_specs=VM,
        compiler_params=params(),
        cost_estimate=cost(0, 2**22),
    )(where, *parts)


def share_of(where, k):
    return ((where[0] + 8 + k) & 7) * SHARE


def last_right_kernel(where, rs_in, s3, rs):
    z, core = where[2] >> 1, where[2] & 1
    for k in range(3):
        prep_right(s3.at[k], rs, ((z + 3 - k) & 3) * 2 + 1 - core)


def last_right(where, rs, s4):
    return pl.pallas_call(
        last_right_kernel,
        out_shape=RIGHT,
        in_specs=[SM, VM, VM],
        out_specs=VM,
        input_output_aliases={1: 0},
        compiler_params=params(),
        cost_estimate=cost(0, 2**22),
    )(where, rs, s4)


def shares(where, tab, ls, rs, offsets, after):
    def kernel(where, tab, ls, rs, after_ref, o_ref):
        for n, k in enumerate(offsets):
            share_into(tab, share_of(where, k), o_ref, n * 512, 8, ls, rs)

    return pl.pallas_call(
        kernel,
        out_shape=jax.ShapeDtypeStruct((512 * len(offsets), 128), F32),
        in_specs=[SM, SM, VM, VM, pl.BlockSpec(memory_space=pl.ANY)],
        out_specs=VM,
        compiler_params=params(),
        cost_estimate=cost(2**27 * len(offsets), 2**20 * len(offsets)),
    )(where, tab, ls, rs, after)


def far_kernel(where, tab, ls, rs, after_ref, f0, f1):
    share_into(tab, share_of(where, 4), f0, 0, 4, ls, rs)
    share_into(tab, share_of(where, 4) + 8, f1, 0, 4, ls, rs)


def far(where, tab, ls, rs, after):
    half = jax.ShapeDtypeStruct((256, 128), F32)
    return pl.pallas_call(
        far_kernel,
        out_shape=(half, half),
        in_specs=[SM, SM, VM, VM, pl.BlockSpec(memory_space=pl.ANY)],
        out_specs=(VM, VM),
        compiler_params=params(),
        cost_estimate=cost(2**27, 2**20),
    )(where, tab, ls, rs, after)


def up_kernel(near, q, half, o_ref):
    o_ref[0:256, :] = near[0:256, :] + q[0:256, :] + half[...]
    o_ref[256:512, :] = near[256:512, :] + q[256:512, :]


def down_kernel(near, q, half, after_ref, o_ref):
    o_ref[0:256, :] = near[512:768, :] + q[0:256, :]
    o_ref[256:512, :] = near[768:1024, :] + q[256:512, :] + half[...]


def merge(kernel, near, q, half, *after, weight):
    return pl.pallas_call(
        kernel,
        out_shape=jax.ShapeDtypeStruct((512, 128), F32),
        in_specs=[VM] * 3 + [pl.BlockSpec(memory_space=pl.ANY)] * len(after),
        out_specs=VM,
        compiler_params=params(),
        cost_estimate=cost(0, weight),
    )(near, q, half, *after)


def sum_kernel(near, q1, q2, u, o_ref):
    o_ref[...] = near[1024:1536, :] + q1[512:1024, :] + q2[512:1024, :] + u[...]


def partial_sum(*a):
    return pl.pallas_call(
        sum_kernel,
        out_shape=jax.ShapeDtypeStruct((512, 128), F32),
        in_specs=[VM] * 4,
        out_specs=VM,
        compiler_params=params(),
        cost_estimate=cost(0, 2**21),
    )(*a)


def last_kernel(part, d, o_ref):
    for p in range(8):
        s = slice(p * 64, (p + 1) * 64)
        v = part[s, :] + d[s, :]
        o_ref[2 * p] = v[:, 0:64]
        o_ref[2 * p + 1] = v[:, 64:128]


def last(part, d):
    return pl.pallas_call(
        last_kernel,
        out_shape=jax.ShapeDtypeStruct((SHARE, BS, BS), F32),
        in_specs=[VM] * 2,
        out_specs=VM,
        compiler_params=params(),
        cost_estimate=cost(0, 2**21),
    )(part, d)


def to_group(x, axis, groups):
    return lax.all_to_all(x, axis, 0, 0, axis_index_groups=groups)


Z_GROUPS = [[z * 4 + c for z in range(3)] for c in range(4)]
X_GROUPS = [[z * 4 + c for c in range(4)] for z in range(3)]


def along_x(x, k):
    return lax.ppermute(x, "col", [(z * 4 + c, z * 4 + (c + k) % 4) for z in range(3) for c in range(4)])


def along_z(x, k):
    return lax.ppermute(x, "row", [(z * 2 + c, (z + k) % 4 * 2 + c) for z in range(4) for c in range(2)])


def swap_core(x):
    return lax.ppermute(x, "row", [(i, i ^ 1) for i in range(8)])


def along_depth(x, k):
    return lax.ppermute(x, "depth", [(i, (i + k) % LAYERS) for i in range(LAYERS)])


def per_device(left_blocks, right_blocks, triples):
    me, col, row = lax.axis_index("depth"), lax.axis_index("col"), lax.axis_index("row")
    where = jnp.stack([me, col, row]).astype(jnp.int32)
    l3, l = pack_left(left_blocks)
    zs = to_group(l3, "col", Z_GROUPS)
    r = pack_right(right_blocks)
    tab = table(triples)
    sibling = swap_core(r)
    ls = split_one(where, 0, l)
    for k in (1, 2, 3):
        ls = split_one(where, k, along_x(l, k), ls)
    zs, ls, sibling, tab, r, where = lax.optimization_barrier((zs, ls, sibling, tab, r, where))
    xs = to_group(spread(where, zs), "col", X_GROUPS)
    rk = [along_z(r, k) for k in (1, 2, 3)]
    ls = split_others(where, ls, xs)
    rk, ls = lax.optimization_barrier((rk, ls))
    s3 = swap_core(jnp.stack(rk))
    rs = last_right(where, first_right(where, r, sibling, *rk), s3)
    p3 = shares(where, tab, ls, rs, (3, 1), where)
    m3 = shares(where, tab, ls, rs, (-3, -1), p3)
    f0, f1 = far(where, tab, ls, rs, m3)
    q1, q2 = along_depth(p3, 1), along_depth(m3, -1)
    q3, q4 = along_depth(f0, 2), along_depth(f1, -2)
    near = shares(where, tab, ls, rs, (2, -2, 0), f0)
    u = merge(up_kernel, near, q1, q3, weight=2**22)
    d = merge(down_kernel, near, q2, q4, u, weight=2**20)
    u, d = along_depth(u, 2), along_depth(d, -2)
    return last(partial_sum(near, q1, q2, u), d)


def solution(mesh):
    placed = (
        P(("row", "col", "depth"), None, None),
        P(("row", "col", "depth"), None, None),
        P(None, ("row", "col", "depth")),
    )
    return jax.shard_map(
        per_device,
        mesh=mesh,
        in_specs=placed,
        out_specs=P(("row", "col", "depth"), None, None),
        check_vma=False,
    )
```

```python
import jax
import jax.numpy as jnp
from jax import lax
from jax.experimental import pallas as pl
from jax.experimental.pallas import tpu as pltpu
from jax.sharding import PartitionSpec as P

BS = 64
GROUPS = 4
SLOTS = 512
PC = 128
LAYERS = 8
SHARE = PC // LAYERS
VM = pl.BlockSpec(memory_space=pltpu.VMEM)
SM = pl.BlockSpec(memory_space=pltpu.SMEM)
F32 = jnp.float32
BF16 = jnp.bfloat16


def params():
    return pltpu.CompilerParams(vmem_limit_bytes=16 * 2**20)


def cost(flops, nbytes):
    return pl.CostEstimate(flops=flops, bytes_accessed=nbytes, transcendentals=0)


def pack_left_kernel(l_ref, three_ref, one_ref):
    for i in range(4):
        for h in range(2):
            v = jnp.concatenate([l_ref[4 * i + 2 * h], l_ref[4 * i + 2 * h + 1]], axis=1)
            at = (slice(i * 64, (i + 1) * 64), slice(h * 128, (h + 1) * 128))
            for c in range(3):
                three_ref[(c,) + at] = v
            one_ref[at] = v


def pack_left(l):
    return pl.pallas_call(
        pack_left_kernel,
        out_shape=(jax.ShapeDtypeStruct((3, 256, 256), F32), jax.ShapeDtypeStruct((256, 256), F32)),
        in_specs=[VM],
        out_specs=(VM, VM),
        compiler_params=params(),
        cost_estimate=cost(0, 2**21),
    )(l)


def pack_right_kernel(r_ref, o_ref):
    for g in range(GROUPS):
        for h in range(2):
            o_ref[g * 64 : (g + 1) * 64, h * 128 : (h + 1) * 128] = jnp.concatenate(
                [r_ref[8 * h + g], r_ref[8 * h + 4 + g]], axis=1
            )


def pack_right(r):
    return pl.pallas_call(
        pack_right_kernel,
        out_shape=jax.ShapeDtypeStruct((256, 256), F32),
        in_specs=[VM],
        out_specs=VM,
        compiler_params=params(),
        cost_estimate=cost(0, 2**21),
    )(r)


def table_kernel(t_ref, o_ref):
    def clear(k, c):
        o_ref[k] = 0
        return c

    lax.fori_loop(0, 136, clear, 0, unroll=8)

    def put(t, c):
        a = t_ref[0, t]
        b = t_ref[1, t]
        k = t_ref[2, t]
        o_ref[k] = o_ref[k] | (a >> 2) | ((b >> 2) << 8) | (1 << (16 + (a & 3)))
        return c

    lax.fori_loop(0, SLOTS, put, 0, unroll=8)


def table(t):
    return pl.pallas_call(
        table_kernel,
        out_shape=jax.ShapeDtypeStruct((136,), jnp.int32),
        in_specs=[SM],
        out_specs=SM, compiler_params=params(),
        cost_estimate=cost(0, 2**23),
    )(t)


def prep_left(x, ls, at):
    for i in range(4):
        v = x[i * 64 : (i + 1) * 64, :]
        hi = v.astype(BF16)
        ls[at * 4 + i, 0:64, :] = hi
        ls[at * 4 + i, 64:128, :] = (v - hi.astype(F32)).astype(BF16)


def prep_right(x, rs, at):
    lane = lax.broadcasted_iota(jnp.int32, (64, 128), 1)
    for h in range(2):
        for g in range(GROUPS):
            v = x[g * 64 : (g + 1) * 64, h * 128 : (h + 1) * 128]
            hi = v.astype(BF16).astype(F32)
            lo = pltpu.roll(v - hi, 64, 1)
            rs[at * 4 + 2 * h, g * 64 : (g + 1) * 64, :] = jnp.where(lane < 64, hi, lo).astype(BF16)
            rs[at * 4 + 2 * h + 1, g * 64 : (g + 1) * 64, :] = jnp.where(lane < 64, lo, hi).astype(BF16)


def one_slot(word, ls, rs):
    i = word & 255
    j = (word >> 8) & 255
    g = lax.broadcasted_iota(jnp.int32, (1, 256), 1) // 64
    used = (((word >> 16) >> g) & 1).astype(F32).astype(BF16)
    p = jnp.dot(ls[i] * used, rs[j], preferred_element_type=F32)
    return p[:64] + p[64:]


def two_slots(k, tab, ls, rs):
    xa = one_slot(tab[k], ls, rs)
    xb = one_slot(tab[k + 1], ls, rs)
    lane = lax.broadcasted_iota(jnp.int32, (64, 128), 1)
    u = jnp.where(lane < 64, xa, xb)
    v = jnp.where(lane < 64, xb, xa)
    return u + pltpu.roll(v, 64, 1)


def share_into(tab, first, o_ref, at, count, ls, rs):
    for n in range(count):
        o_ref[at + n * 64 : at + (n + 1) * 64, :] = two_slots(first + 2 * n, tab, ls, rs)


LEFT = jax.ShapeDtypeStruct((48, 128, 256), BF16)
RIGHT = jax.ShapeDtypeStruct((32, 256, 128), BF16)


def split_one(where, k, part, *so_far):
    def kernel(where, part, *rest):
        z, x = where[1] >> 2, where[1] & 3
        prep_left(part, rest[-1], z * 4 + ((x + 4 - k) & 3))

    return pl.pallas_call(
        kernel,
        out_shape=LEFT,
        in_specs=[SM] + [VM] * (1 + len(so_far)),
        out_specs=VM,
        input_output_aliases={2: 0} if so_far else {},
        compiler_params=params(),
        cost_estimate=cost(0, 2**20),
    )(where, part, *so_far)


def spread_kernel(where, zs, o_ref):
    z = where[1] >> 2
    for h in range(2):
        at = lax.rem(z + 1 + h, 3)
        for q in range(4):
            v = zs[at, q * 64 : (q + 1) * 64, :]
            for c in range(4):
                o_ref[c, h * 256 + q * 64 : h * 256 + (q + 1) * 64, :] = v


def spread(where, zs):
    return pl.pallas_call(
        spread_kernel,
        out_shape=jax.ShapeDtypeStruct((4, 512, 256), F32),
        in_specs=[SM, VM],
        out_specs=VM,
        compiler_params=params(),
        cost_estimate=cost(0, 2**21),
    )(where, zs)


def split_others_kernel(where, ls_in, xs, ls):
    z = where[1] >> 2
    for c in range(4):
        for h in range(2):
            prep_left(xs.at[c, pl.ds(h * 256, 256)], ls, lax.rem(z + 1 + h, 3) * 4 + c)


def split_others(where, ls, xs):
    return pl.pallas_call(
        split_others_kernel,
        out_shape=LEFT,
        in_specs=[SM, VM, VM],
        out_specs=VM,
        input_output_aliases={1: 0},
        compiler_params=params(),
        cost_estimate=cost(0, 2**22),
    )(where, ls, xs)


def first_right_kernel(where, r, sibling, r1, r2, s1, s2, rs):
    z, core = where[2] >> 1, where[2] & 1
    prep_right(r, rs, z * 2 + core)
    prep_right(sibling, rs, z * 2 + 1 - core)
    prep_right(r1, rs, (z ^ 1) * 2 + core)
    prep_right(r2, rs, (z ^ 2) * 2 + core)
    prep_right(s1, rs, (z ^ 1) * 2 + 1 - core)
    prep_right(s2, rs, (z ^ 2) * 2 + 1 - core)


def first_right(where, *parts):
    return pl.pallas_call(
        first_right_kernel,
        out_shape=RIGHT,
        in_specs=[SM] + [VM] * 6,
        out_specs=VM,
        compiler_params=params(),
        cost_estimate=cost(0, 2**22),
    )(where, *parts)


def share_of(where, k):
    return ((where[0] + 8 + k) & 7) * SHARE


def last_right_kernel(where, rs_in, r3, s3, rs):
    z, core = where[2] >> 1, where[2] & 1
    prep_right(r3, rs, (z ^ 3) * 2 + core)
    prep_right(s3, rs, (z ^ 3) * 2 + 1 - core)


def last_right(where, rs, r3, s3):
    return pl.pallas_call(
        last_right_kernel,
        out_shape=RIGHT,
        in_specs=[SM, VM, VM, VM],
        out_specs=VM,
        input_output_aliases={1: 0},
        compiler_params=params(),
        cost_estimate=cost(0, 2**21),
    )(where, rs, r3, s3)


def shares(where, tab, ls, rs, offsets, after):
    def kernel(where, tab, ls, rs, after_ref, o_ref):
        for n, k in enumerate(offsets):
            share_into(tab, share_of(where, k), o_ref, n * 512, 8, ls, rs)

    return pl.pallas_call(
        kernel,
        out_shape=jax.ShapeDtypeStruct((512 * len(offsets), 128), F32),
        in_specs=[SM, SM, VM, VM, pl.BlockSpec(memory_space=pl.ANY)],
        out_specs=VM,
        compiler_params=params(),
        cost_estimate=cost(2**27 * len(offsets), 2**20 * len(offsets)),
    )(where, tab, ls, rs, after)


def far_kernel(where, tab, ls, rs, after_ref, f0, f1):
    share_into(tab, share_of(where, 4), f0, 0, 4, ls, rs)
    share_into(tab, share_of(where, 4) + 8, f1, 0, 4, ls, rs)


def far(where, tab, ls, rs, after):
    half = jax.ShapeDtypeStruct((256, 128), F32)
    return pl.pallas_call(
        far_kernel,
        out_shape=(half, half),
        in_specs=[SM, SM, VM, VM, pl.BlockSpec(memory_space=pl.ANY)],
        out_specs=(VM, VM),
        compiler_params=params(),
        cost_estimate=cost(2**27, 2**20),
    )(where, tab, ls, rs, after)


def up_kernel(near, q, half, o_ref):
    o_ref[0:256, :] = near[0:256, :] + q[0:256, :] + half[...]
    o_ref[256:512, :] = near[256:512, :] + q[256:512, :]


def down_kernel(near, q, half, after_ref, o_ref):
    o_ref[0:256, :] = near[512:768, :] + q[0:256, :]
    o_ref[256:512, :] = near[768:1024, :] + q[256:512, :] + half[...]


def merge(kernel, near, q, half, *after, weight):
    return pl.pallas_call(
        kernel,
        out_shape=jax.ShapeDtypeStruct((512, 128), F32),
        in_specs=[VM] * 3 + [pl.BlockSpec(memory_space=pl.ANY)] * len(after),
        out_specs=VM,
        compiler_params=params(),
        cost_estimate=cost(0, weight),
    )(near, q, half, *after)


def sum_kernel(near, q1, q2, u, o_ref):
    o_ref[...] = near[1024:1536, :] + q1[512:1024, :] + q2[512:1024, :] + u[...]


def partial_sum(*a):
    return pl.pallas_call(
        sum_kernel,
        out_shape=jax.ShapeDtypeStruct((512, 128), F32),
        in_specs=[VM] * 4,
        out_specs=VM,
        compiler_params=params(),
        cost_estimate=cost(0, 2**21),
    )(*a)


def last_kernel(part, d, o_ref):
    for p in range(8):
        s = slice(p * 64, (p + 1) * 64)
        v = part[s, :] + d[s, :]
        o_ref[2 * p] = v[:, 0:64]
        o_ref[2 * p + 1] = v[:, 64:128]


def last(part, d):
    return pl.pallas_call(
        last_kernel,
        out_shape=jax.ShapeDtypeStruct((SHARE, BS, BS), F32),
        in_specs=[VM] * 2,
        out_specs=VM,
        compiler_params=params(),
        cost_estimate=cost(0, 2**21),
    )(part, d)


def to_group(x, axis, groups):
    return lax.all_to_all(x, axis, 0, 0, axis_index_groups=groups)


Z_GROUPS = [[z * 4 + c for z in range(3)] for c in range(4)]
X_GROUPS = [[z * 4 + c for c in range(4)] for z in range(3)]


def along_x(x, k):
    return lax.ppermute(x, "col", [(z * 4 + c, z * 4 + (c + k) % 4) for z in range(3) for c in range(4)])


def swap_z(x, k):
    return lax.ppermute(x, "row", [(i, i ^ (2 * k)) for i in range(8)])


def swap_core(x):
    return lax.ppermute(x, "row", [(i, i ^ 1) for i in range(8)])


def along_depth(x, k):
    return lax.ppermute(x, "depth", [(i, (i + k) % LAYERS) for i in range(LAYERS)])


def per_device(left_blocks, right_blocks, triples):
    me, col, row = lax.axis_index("depth"), lax.axis_index("col"), lax.axis_index("row")
    where = jnp.stack([me, col, row]).astype(jnp.int32)
    l3, l = pack_left(left_blocks)
    zs = to_group(l3, "col", Z_GROUPS)
    r = pack_right(right_blocks)
    tab = table(triples)
    sibling = swap_core(r)
    ls = split_one(where, 0, l)
    for k in (1, 2, 3):
        ls = split_one(where, k, along_x(l, k), ls)
    zs, ls, sibling, tab, r, where = lax.optimization_barrier((zs, ls, sibling, tab, r, where))
    xs = to_group(spread(where, zs), "col", X_GROUPS)
    r2, r1 = swap_z(r, 2), swap_z(r, 1)
    r3 = swap_z(r2, 1)
    s1, s2 = swap_core(r1), swap_core(r2)
    ls = split_others(where, ls, xs)
    r3, ls = lax.optimization_barrier((r3, ls))
    rs = first_right(where, r, sibling, r1, r2, s1, s2)
    rs = last_right(where, rs, r3, swap_core(r3))
    p3 = shares(where, tab, ls, rs, (3, 1), where)
    m3 = shares(where, tab, ls, rs, (-3, -1), p3)
    f0, f1 = far(where, tab, ls, rs, m3)
    q1, q2 = along_depth(p3, 1), along_depth(m3, -1)
    q3, q4 = along_depth(f0, 2), along_depth(f1, -2)
    near = shares(where, tab, ls, rs, (2, -2, 0), f0)
    u = merge(up_kernel, near, q1, q3, weight=2**22)
    d = merge(down_kernel, near, q2, q4, u, weight=2**20)
    u, d = along_depth(u, 2), along_depth(d, -2)
    return last(partial_sum(near, q1, q2, u), d)


def solution(mesh):
    placed = (
        P(("row", "col", "depth"), None, None),
        P(("row", "col", "depth"), None, None),
        P(None, ("row", "col", "depth")),
    )
    return jax.shard_map(
        per_device,
        mesh=mesh,
        in_specs=placed,
        out_specs=P(("row", "col", "depth"), None, None),
        check_vma=False,
    )
```

```python
import jax
import jax.numpy as jnp
from jax import lax
from jax.experimental import pallas as pl
from jax.experimental.pallas import tpu as pltpu
from jax.sharding import PartitionSpec as P

BS = 64
GROUPS = 4
SLOTS = 512
PC = 128
LAYERS = 8
SHARE = PC // LAYERS
VM = pl.BlockSpec(memory_space=pltpu.VMEM)
SM = pl.BlockSpec(memory_space=pltpu.SMEM)
F32 = jnp.float32
BF16 = jnp.bfloat16


def params():
    return pltpu.CompilerParams(vmem_limit_bytes=16 * 2**20)


def cost(flops, nbytes):
    return pl.CostEstimate(flops=flops, bytes_accessed=nbytes, transcendentals=0)


def pack_left_kernel(l_ref, three_ref, one_ref):
    for i in range(4):
        for h in range(2):
            v = jnp.concatenate([l_ref[4 * i + 2 * h], l_ref[4 * i + 2 * h + 1]], axis=1)
            at = (slice(i * 64, (i + 1) * 64), slice(h * 128, (h + 1) * 128))
            for c in range(3):
                three_ref[(c,) + at] = v
            one_ref[at] = v


def pack_left(l):
    return pl.pallas_call(
        pack_left_kernel,
        out_shape=(jax.ShapeDtypeStruct((3, 256, 256), F32), jax.ShapeDtypeStruct((256, 256), F32)),
        in_specs=[VM],
        out_specs=(VM, VM),
        compiler_params=params(),
        cost_estimate=cost(0, 2**21),
    )(l)


def pack_right_kernel(r_ref, o_ref):
    for g in range(GROUPS):
        for h in range(2):
            o_ref[g * 64 : (g + 1) * 64, h * 128 : (h + 1) * 128] = jnp.concatenate(
                [r_ref[8 * h + g], r_ref[8 * h + 4 + g]], axis=1
            )


def pack_right(r):
    return pl.pallas_call(
        pack_right_kernel,
        out_shape=jax.ShapeDtypeStruct((256, 256), F32),
        in_specs=[VM],
        out_specs=VM,
        compiler_params=params(),
        cost_estimate=cost(0, 2**21),
    )(r)


def table_kernel(t_ref, o_ref):
    def clear(k, c):
        o_ref[k] = 0
        return c

    lax.fori_loop(0, 136, clear, 0, unroll=8)

    def put(t, c):
        a = t_ref[0, t]
        b = t_ref[1, t]
        k = t_ref[2, t]
        o_ref[k] = o_ref[k] | (a >> 2) | ((b >> 2) << 8) | (1 << (16 + (a & 3)))
        return c

    lax.fori_loop(0, SLOTS, put, 0, unroll=8)


def table(t):
    return pl.pallas_call(
        table_kernel,
        out_shape=jax.ShapeDtypeStruct((136,), jnp.int32),
        in_specs=[SM],
        out_specs=SM, compiler_params=params(),
        cost_estimate=cost(0, 2**23),
    )(t)


def prep_left(x, ls, at):
    for i in range(4):
        v = x[i * 64 : (i + 1) * 64, :]
        hi = v.astype(BF16)
        ls[at * 4 + i, 0:64, :] = hi
        ls[at * 4 + i, 64:128, :] = (v - hi.astype(F32)).astype(BF16)


def prep_right(x, rs, at):
    lane = lax.broadcasted_iota(jnp.int32, (64, 128), 1)
    for h in range(2):
        for g in range(GROUPS):
            v = x[g * 64 : (g + 1) * 64, h * 128 : (h + 1) * 128]
            hi = v.astype(BF16).astype(F32)
            lo = pltpu.roll(v - hi, 64, 1)
            rs[at * 4 + 2 * h, g * 64 : (g + 1) * 64, :] = jnp.where(lane < 64, hi, lo).astype(BF16)
            rs[at * 4 + 2 * h + 1, g * 64 : (g + 1) * 64, :] = jnp.where(lane < 64, lo, hi).astype(BF16)


def one_slot(word, ls, rs):
    i = word & 255
    j = (word >> 8) & 255
    g = lax.broadcasted_iota(jnp.int32, (1, 256), 1) // 64
    used = (((word >> 16) >> g) & 1).astype(F32).astype(BF16)
    p = jnp.dot(ls[i] * used, rs[j], preferred_element_type=F32)
    return p[:64] + p[64:]


def two_slots(k, tab, ls, rs):
    xa = one_slot(tab[k], ls, rs)
    xb = one_slot(tab[k + 1], ls, rs)
    lane = lax.broadcasted_iota(jnp.int32, (64, 128), 1)
    u = jnp.where(lane < 64, xa, xb)
    v = jnp.where(lane < 64, xb, xa)
    return u + pltpu.roll(v, 64, 1)


def share_into(tab, first, o_ref, at, count, ls, rs):
    for n in range(count):
        o_ref[at + n * 64 : at + (n + 1) * 64, :] = two_slots(first + 2 * n, tab, ls, rs)


LEFT = jax.ShapeDtypeStruct((48, 128, 256), BF16)
RIGHT = jax.ShapeDtypeStruct((32, 256, 128), BF16)


def split_one(where, k, part, *so_far):
    def kernel(where, part, *rest):
        z, x = where[1] >> 2, where[1] & 3
        prep_left(part, rest[-1], z * 4 + ((x + 4 - k) & 3))

    return pl.pallas_call(
        kernel,
        out_shape=LEFT,
        in_specs=[SM] + [VM] * (1 + len(so_far)),
        out_specs=VM,
        input_output_aliases={2: 0} if so_far else {},
        compiler_params=params(),
        cost_estimate=cost(0, 2**20),
    )(where, part, *so_far)


def spread_kernel(where, zs, o_ref):
    z = where[1] >> 2
    for h in range(2):
        at = lax.rem(z + 1 + h, 3)
        for q in range(4):
            v = zs[at, q * 64 : (q + 1) * 64, :]
            for c in range(4):
                o_ref[c, h * 256 + q * 64 : h * 256 + (q + 1) * 64, :] = v


def spread(where, zs):
    return pl.pallas_call(
        spread_kernel,
        out_shape=jax.ShapeDtypeStruct((4, 512, 256), F32),
        in_specs=[SM, VM],
        out_specs=VM,
        compiler_params=params(),
        cost_estimate=cost(0, 2**21),
    )(where, zs)


def split_others_kernel(where, ls_in, xs, ls):
    z = where[1] >> 2
    for c in range(4):
        for h in range(2):
            prep_left(xs.at[c, pl.ds(h * 256, 256)], ls, lax.rem(z + 1 + h, 3) * 4 + c)


def split_others(where, ls, xs):
    return pl.pallas_call(
        split_others_kernel,
        out_shape=LEFT,
        in_specs=[SM, VM, VM],
        out_specs=VM,
        input_output_aliases={1: 0},
        compiler_params=params(),
        cost_estimate=cost(0, 2**22),
    )(where, ls, xs)


def first_right_kernel(where, r, sibling, r1, r2, s1, s2, rs):
    z, core = where[2] >> 1, where[2] & 1
    prep_right(r, rs, z * 2 + core)
    prep_right(sibling, rs, z * 2 + 1 - core)
    prep_right(r1, rs, (z ^ 1) * 2 + core)
    prep_right(r2, rs, (z ^ 2) * 2 + core)
    prep_right(s1, rs, (z ^ 1) * 2 + 1 - core)
    prep_right(s2, rs, (z ^ 2) * 2 + 1 - core)


def first_right(where, *parts):
    return pl.pallas_call(
        first_right_kernel,
        out_shape=RIGHT,
        in_specs=[SM] + [VM] * 6,
        out_specs=VM,
        compiler_params=params(),
        cost_estimate=cost(0, 2**22),
    )(where, *parts)


def share_of(where, k):
    return ((where[0] + 8 + k) & 7) * SHARE


def last_right_kernel(where, rs_in, r3, s3, rs):
    z, core = where[2] >> 1, where[2] & 1
    prep_right(r3, rs, (z ^ 3) * 2 + core)
    prep_right(s3, rs, (z ^ 3) * 2 + 1 - core)


def last_right(where, rs, r3, s3):
    return pl.pallas_call(
        last_right_kernel,
        out_shape=RIGHT,
        in_specs=[SM, VM, VM, VM],
        out_specs=VM,
        input_output_aliases={1: 0},
        compiler_params=params(),
        cost_estimate=cost(0, 2**21),
    )(where, rs, r3, s3)


def shares(where, tab, ls, rs, offsets, after):
    def kernel(where, tab, ls, rs, after_ref, o_ref):
        for n, k in enumerate(offsets):
            share_into(tab, share_of(where, k), o_ref, n * 512, 8, ls, rs)

    return pl.pallas_call(
        kernel,
        out_shape=jax.ShapeDtypeStruct((512 * len(offsets), 128), F32),
        in_specs=[SM, SM, VM, VM, pl.BlockSpec(memory_space=pl.ANY)],
        out_specs=VM,
        compiler_params=params(),
        cost_estimate=cost(2**27 * len(offsets), 2**20 * len(offsets)),
    )(where, tab, ls, rs, after)


def far_kernel(where, tab, ls, rs, after_ref, f0, f1):
    share_into(tab, share_of(where, 4), f0, 0, 4, ls, rs)
    share_into(tab, share_of(where, 4) + 8, f1, 0, 4, ls, rs)


def far(where, tab, ls, rs, after):
    half = jax.ShapeDtypeStruct((256, 128), F32)
    return pl.pallas_call(
        far_kernel,
        out_shape=(half, half),
        in_specs=[SM, SM, VM, VM, pl.BlockSpec(memory_space=pl.ANY)],
        out_specs=(VM, VM),
        compiler_params=params(),
        cost_estimate=cost(2**27, 2**20),
    )(where, tab, ls, rs, after)


def up_kernel(near, q, half, o_ref):
    o_ref[0:256, :] = near[0:256, :] + q[0:256, :] + half[...]
    o_ref[256:512, :] = near[256:512, :] + q[256:512, :]


def down_kernel(near, q, half, after_ref, o_ref):
    o_ref[0:256, :] = near[512:768, :] + q[0:256, :]
    o_ref[256:512, :] = near[768:1024, :] + q[256:512, :] + half[...]


def merge(kernel, near, q, half, *after, weight):
    return pl.pallas_call(
        kernel,
        out_shape=jax.ShapeDtypeStruct((512, 128), F32),
        in_specs=[VM] * 3 + [pl.BlockSpec(memory_space=pl.ANY)] * len(after),
        out_specs=VM,
        compiler_params=params(),
        cost_estimate=cost(0, weight),
    )(near, q, half, *after)


def sum_kernel(near, q1, q2, u, o_ref):
    o_ref[...] = near[1024:1536, :] + q1[512:1024, :] + q2[512:1024, :] + u[...]


def partial_sum(*a):
    return pl.pallas_call(
        sum_kernel,
        out_shape=jax.ShapeDtypeStruct((512, 128), F32),
        in_specs=[VM] * 4,
        out_specs=VM,
        compiler_params=params(),
        cost_estimate=cost(0, 2**21),
    )(*a)


def last_kernel(part, d, o_ref):
    for p in range(8):
        s = slice(p * 64, (p + 1) * 64)
        v = part[s, :] + d[s, :]
        o_ref[2 * p] = v[:, 0:64]
        o_ref[2 * p + 1] = v[:, 64:128]


def last(part, d):
    return pl.pallas_call(
        last_kernel,
        out_shape=jax.ShapeDtypeStruct((SHARE, BS, BS), F32),
        in_specs=[VM] * 2,
        out_specs=VM,
        compiler_params=params(),
        cost_estimate=cost(0, 2**21),
    )(part, d)


def to_group(x, axis, groups):
    return lax.all_to_all(x, axis, 0, 0, axis_index_groups=groups)


Z_GROUPS = [[z * 4 + c for z in range(3)] for c in range(4)]
X_GROUPS = [[z * 4 + c for c in range(4)] for z in range(3)]


def along_x(x, k):
    return lax.ppermute(x, "col", [(z * 4 + c, z * 4 + (c + k) % 4) for z in range(3) for c in range(4)])


def swap_z(x, k):
    return lax.ppermute(x, "row", [(i, i ^ (2 * k)) for i in range(8)])


def swap_core(x):
    return lax.ppermute(x, "row", [(i, i ^ 1) for i in range(8)])


def along_depth(x, k):
    return lax.ppermute(x, "depth", [(i, (i + k) % LAYERS) for i in range(LAYERS)])


def per_device(left_blocks, right_blocks, triples):
    me, col, row = lax.axis_index("depth"), lax.axis_index("col"), lax.axis_index("row")
    where = jnp.stack([me, col, row]).astype(jnp.int32)
    l3, l = pack_left(left_blocks)
    zs = to_group(l3, "col", Z_GROUPS)
    r = pack_right(right_blocks)
    tab = table(triples)
    sibling = swap_core(r)
    ls = split_one(where, 0, l)
    for k in (1, 2, 3):
        ls = split_one(where, k, along_x(l, k), ls)
    zs, ls, sibling, tab, r, where = lax.optimization_barrier((zs, ls, sibling, tab, r, where))
    xs = to_group(spread(where, zs), "col", X_GROUPS)
    r2, r1 = swap_z(r, 2), swap_z(r, 1)
    r3 = swap_z(r2, 1)
    s1, s2 = swap_core(r1), swap_core(r2)
    ls = split_others(where, ls, xs)
    s3 = swap_core(r3)
    s2, ls = lax.optimization_barrier((s2, ls))
    rs = first_right(where, r, sibling, r1, r2, s1, s2)
    rs = last_right(where, rs, r3, s3)
    p3 = shares(where, tab, ls, rs, (3, 1), where)
    m3 = shares(where, tab, ls, rs, (-3, -1), p3)
    f0, f1 = far(where, tab, ls, rs, m3)
    q1, q2 = along_depth(p3, 1), along_depth(m3, -1)
    q3, q4 = along_depth(f0, 2), along_depth(f1, -2)
    near = shares(where, tab, ls, rs, (2, -2, 0), f0)
    u = merge(up_kernel, near, q1, q3, weight=2**22)
    d = merge(down_kernel, near, q2, q4, u, weight=2**20)
    u, d = along_depth(u, 2), along_depth(d, -2)
    return last(partial_sum(near, q1, q2, u), d)


def solution(mesh):
    placed = (
        P(("row", "col", "depth"), None, None),
        P(("row", "col", "depth"), None, None),
        P(None, ("row", "col", "depth")),
    )
    return jax.shard_map(
        per_device,
        mesh=mesh,
        in_specs=placed,
        out_specs=P(("row", "col", "depth"), None, None),
        check_vma=False,
    )
```
